512 devices in a mesh: seq: 64 (over z, x, core), head: 8 (over y).
Axes of the slice: x: 4, y: 8, z: 8, core: 2. Of those that a mesh axis runs over, the one named last changes fastest.
Arguments:
- queries: bfloat16 [24576, 4096], P('seq', 'head'), may hold values from -8 to 8
- keys: bfloat16 [24576, 4096], P('seq', 'head'), may hold values from -8 to 8
- values: bfloat16 [24576, 4096], P('seq', 'head'), may hold values from -6 to 6
- target_row: int32 [24576], P('seq'), may hold values from 0 to 24575, as said below
- doc_lengths: int32 [128], replicated, may hold values from 0 to 768, as said below
Outputs:
- mixed: bfloat16 [24576, 4096], P('seq', 'head')
The draws below stay inside these ranges and needn't reach their ends.
Inputs may be any that keep to these rules, and one draw needn't show every extreme that they name: `target_row`: A permutation of the rows. The rows of one device go to at most 9 rows of any one device's block of 384 rows in document order, and every device sends exactly 9 rows to some device. `doc_lengths`: they sum to 24576; zero lengths occur; no document crosses a multiple of 768 rows, and some document fills the rows between two such multiples.
All inputs are finite; a program needn't handle non-finite values.
Results may differ from the reference program's by a relative error of at most 0.0035.
Values may be sent and summed in bfloat16 or wider, within the bound.
A program may use at most 64 MiB of HBM per device.

```python
import math
import jax
import jax.numpy as jnp
from jax import lax

HEADS = 32
HD = 128
ROWS_DEV = 384
GROUP = 4
TOKENS = 24576


def draw_queries(key, part):
    key = jax.random.fold_in(key, 31)
    first_key = jax.random.fold_in(key, 0)
    noise = jax.random.normal(first_key, (TOKENS, HEADS * HD), jnp.float32)
    return jnp.clip(noise, -6.0, 6.0).astype(jnp.bfloat16)


def draw_keys(key, part):
    key = jax.random.fold_in(key, 37)
    noise = jax.random.normal(key, (TOKENS, HEADS * HD), jnp.float32)
    return jnp.clip(noise, -6.0, 6.0).astype(jnp.bfloat16)


def draw_target_row(key, part):
    key = jax.random.fold_in(key, 11)
    count = TOKENS // ROWS_DEV
    rows = ROWS_DEV
    base_count = rows // count
    extra = base_count // 2
    first_key, second_key, third_key = jax.random.split(key, 3)
    sigma = jax.random.permutation(first_key, count).astype(jnp.int32)
    tau = jnp.roll(sigma, -1)
    devices = jnp.arange(count, dtype=jnp.int32)
    counts = base_count + extra * ((devices[None, :] == sigma[:, None]).astype(jnp.int32) - (devices[None, :] == tau[:, None]).astype(jnp.int32))
    row_cum = jnp.cumsum(counts, axis=1)
    positions = jnp.arange(rows, dtype=jnp.int32)
    target_device = jnp.sum((row_cum[:, None, :] <= positions[None, :, None]).astype(jnp.int32), axis=2)
    row_start = row_cum - counts
    within = positions[None, :] - jnp.take_along_axis(row_start, target_device, axis=1)
    col_start = jnp.cumsum(counts, axis=0) - counts
    rank = jnp.take_along_axis(col_start, target_device, axis=1) + within
    perm_target = jax.vmap(lambda each: jax.random.permutation(each, rows))(jax.random.split(second_key, count)).astype(jnp.int32)
    perm_loader = jax.vmap(lambda each: jax.random.permutation(each, rows))(jax.random.split(third_key, count)).astype(jnp.int32)
    target_place = target_device * rows + perm_target[target_device, rank]
    loader_place = devices[:, None] * rows + perm_loader
    result = jnp.zeros((count * rows,), jnp.int32).at[loader_place.reshape(-1)].set(target_place.reshape(-1))
    return result


def draw_doc_lengths(key, part):
    key = jax.random.fold_in(key, 23)
    count = TOKENS // ROWS_DEV
    rows = ROWS_DEV
    half = rows // 2
    half_group = GROUP // 2
    keys_list = jax.random.split(key, 5)
    devices = jnp.arange(count, dtype=jnp.int32)
    first = devices * rows + jax.random.randint(keys_list[0], (count,), 0, half, jnp.int32)
    second = devices * rows + half + jax.random.randint(keys_list[1], (count,), 0, half, jnp.int32)
    on_first = jax.random.randint(keys_list[2], (count,), 0, 2, jnp.int32)
    on_second = jax.random.randint(keys_list[3], (count,), 0, 2, jnp.int32)
    full_half = jax.random.randint(keys_list[4], (), 0, 2 * (count // GROUP), jnp.int32)
    starting = devices % half_group == 0
    first = jnp.where(starting, devices * rows, first)
    keep_first = jnp.where(starting, 1, on_first)
    candidates = jnp.stack([first, second], axis=1).reshape(-1)
    keeping = jnp.stack([keep_first, on_second], axis=1).reshape(-1)
    entries = jnp.arange(2 * count, dtype=jnp.int32)
    entry_half = entries // (2 * half_group)
    in_full = entry_half == full_half
    half_start = entry_half * (half_group * rows)
    candidates = jnp.where(in_full, half_start, candidates)
    keeping = jnp.where(in_full, (entries % (2 * half_group) == 0).astype(jnp.int32), keeping)
    bounds = lax.cummax(jnp.where(keeping == 1, candidates, 0), axis=0)
    ends = jnp.concatenate([bounds[1:], jnp.full((1,), count * rows, jnp.int32)])
    return (ends - bounds).astype(jnp.int32)


def level_of(own_key, extent, cuts, smallest, top_value):
    factor_of = 1.0
    for position, blocks in cuts:
        steps = jax.random.uniform(jax.random.fold_in(jax.random.fold_in(own_key, 6), position), (blocks,), jnp.float32, smallest / len(cuts), top_value / len(cuts))
        factor_of = factor_of * jnp.repeat(jnp.exp(steps), extent[position] // blocks).reshape((-1,) + (1,) * (len(extent) - 1 - position))
    return factor_of


def bell_draw(own_key, shape, scale, limit, cuts=(), kind=jnp.bfloat16):
    values = jax.random.normal(own_key, shape, jnp.float32) * scale
    if len(cuts) > 0:
        values = level_of(own_key, shape, cuts, -0.22, 0.18) * values
    return jnp.clip(values, min=-limit, max=limit).astype(kind)


def setup_inputs(seed: int = 0) -> dict:
    streams_of = jax.random.split(jax.random.key(seed), 6)
    queries = draw_queries(jax.random.fold_in(streams_of[5], 71), 0)
    keys = draw_keys(jax.random.fold_in(streams_of[5], 71), 0)
    values = bell_draw(streams_of[2], (TOKENS, HEADS * HD), 1.0, 6.0, ((0, 64), (1, 8)))
    target_row = draw_target_row(jax.random.fold_in(streams_of[5], 71), 0)
    doc_lengths = draw_doc_lengths(jax.random.fold_in(streams_of[5], 71), 0)
    return dict(queries=queries, keys=keys, values=values, target_row=target_row, doc_lengths=doc_lengths)


def reference(queries, keys, values, target_row, doc_lengths):
    width = HEADS * HD
    span = GROUP * ROWS_DEV
    groups = TOKENS // span
    scale = 1.0 / math.sqrt(HD)

    def place(source):
        return jnp.zeros((TOKENS, width), source.dtype).at[target_row].set(source)
    q_rows = place(queries)
    k_rows = place(keys)
    v_rows = place(values)
    starts = jnp.cumsum(doc_lengths) - doc_lengths

    def one_group(index):
        first = index * span
        query_group = lax.dynamic_slice_in_dim(q_rows, first, span, 0).reshape(span, HEADS, HD)
        key_group = lax.dynamic_slice_in_dim(k_rows, first, span, 0).reshape(span, HEADS, HD)
        value_group = lax.dynamic_slice_in_dim(v_rows, first, span, 0).reshape(span, HEADS, HD)
        positions = first + jnp.arange(span, dtype=jnp.int32)
        labels = lax.optimization_barrier(jnp.sum((starts[None, :] <= positions[:, None]).astype(jnp.int32), axis=1))

        def one_head(head):
            query_head = lax.dynamic_index_in_dim(query_group, head, 1, keepdims=False)
            key_head = lax.dynamic_index_in_dim(key_group, head, 1, keepdims=False)
            value_head = lax.dynamic_index_in_dim(value_group, head, 1, keepdims=False)
            pieces = []
            for block in range(span // 512):
                lower = block * 512
                upper = lower + 512
                scores = jnp.dot(query_head[lower:upper], key_head[:upper].T, preferred_element_type=jnp.float32) * scale
                allowed = (labels[lower:upper, None] == labels[None, :upper]) & (positions[None, :upper] <= positions[lower:upper, None])
                scores = jnp.where(allowed, scores, -1e+30)
                top = lax.optimization_barrier(jnp.max(scores, axis=1, keepdims=True))
                weights = jnp.where(allowed, jnp.exp(scores - top), 0.0)
                total = lax.optimization_barrier(jnp.sum(weights, axis=1, keepdims=True))
                mixed = jnp.dot(weights.astype(jnp.bfloat16), value_head[:upper], preferred_element_type=jnp.float32) / total
                pieces.append(mixed.astype(jnp.bfloat16))
            return jnp.concatenate(pieces, axis=0)
        heads_out = lax.map(one_head, jnp.arange(HEADS, dtype=jnp.int32))
        return jnp.transpose(heads_out, (1, 0, 2)).reshape(span, width)
    result = lax.map(one_group, jnp.arange(groups, dtype=jnp.int32))
    return result.reshape(TOKENS, width)
```

```python
import functools
import math

import jax
import jax.numpy as jnp
from jax import lax
from jax.experimental import pallas as pl
from jax.experimental.pallas import tpu as pltpu
from jax.sharding import PartitionSpec as P

HD = 128
ROWS = 384
CAP = 9
CHIP = 2 * ROWS
NZ, NX = 8, 4
NEG = -1e30
MESH = pl.DeviceIdType.MESH
BF = jnp.bfloat16
F32 = jnp.float32
I32 = jnp.int32
WIDE = 7 * HD
NT = (((1,), (1,)), ((), ()))


def iota(shape, dim):
    return lax.broadcasted_iota(I32, shape, dim)


def kernel(q_ref, k_ref, v_ref, t_ref, len_ref, out_ref, send, recv, placed, bias, dense, mixed, send_sem, recv_sem, swap_send, swap_recv):
    me = lax.axis_index("seq")
    head = lax.axis_index("head")
    z, x, c = me // 8, (me // 2) % 4, me % 2

    def peer(k):
        rz, rx, xc = k // 8, (k // 2) % 4, k % 2
        return (((z + rz) % 8) * 8 + ((x + rx) % 4) * 2 + (c + xc) % 2, head)

    barrier = pltpu.get_barrier_semaphore()
    for k in range(1, 64):
        pl.semaphore_signal(barrier, inc=1, device_id=peer(k), device_id_type=MESH)

    t = t_ref[...]
    dev = jnp.floor((t.astype(F32) + 0.5) * (1.0 / ROWS)).astype(I32)
    local = t - dev * ROWS
    rzv = ((dev >> 3) - z) & 7
    rxv = (((dev >> 1) & 3) - x) & 3
    cc = dev & 1
    m = rzv * 4 + rxv
    flags = iota((64, ROWS), 0) == m * 2 + cc
    before = (iota((ROWS, ROWS), 0) < iota((ROWS, ROWS), 1)).astype(BF)
    cum = jnp.dot(flags.astype(F32).astype(BF), before, preferred_element_type=F32)
    rank = jnp.sum(jnp.where(flags, cum, 0.0), axis=0, keepdims=True).astype(I32)
    s = cc * CAP + rank
    place = cc * ROWS + local
    hi, lo = ((place >> 4) + 1).astype(F32), (place & 15).astype(F32)
    over = s >= 16
    main_row = jnp.where(over, -1, m * 16 + s)
    left_row = jnp.where(over, m * 16 + s - 16, -1000)
    place_row = m * 16 + jnp.where(over, 14, 12)
    lanes = iota((HD, ROWS), 0)
    hot = []
    for core in range(2):
        kk = rxv * 2 + ((c + core) & 1)
        main_hot = lanes == kk * 16 + s
        left_hot = ((lanes >> 4) == kk) & ((lanes & 15) < 12) & ((lanes & 1) == s - 16)
        hot.append(jnp.where(over, left_hot.astype(F32), main_hot.astype(F32)).astype(BF))
    hot = jnp.concatenate(hot, axis=0)

    copies = {}

    def build(chunk):
        rows = iota((256, ROWS), 0) + chunk * 256
        pick = (rows == main_row).astype(F32).astype(BF)
        at = pl.ds(chunk * 16, 16)
        left = lax.dot_general(
            (jnp.where(rows == place_row, hi, 0.0) + jnp.where(rows == place_row + 1, lo, 0.0)).astype(BF),
            hot, NT, preferred_element_type=F32)
        for a, ref in enumerate((q_ref, k_ref, v_ref)):
            got = jnp.dot(pick, ref[...], preferred_element_type=F32).astype(BF)
            for core in range(2):
                send[at, core, :, a * 256:(a + 1) * 256] = got[:, core * 256:(core + 1) * 256].reshape(16, 16, 256)
            for j in range(2):
                b = a * 2 + j
                pick_left = (rows - 2 * b == left_row).astype(F32).astype(BF)
                both = jnp.concatenate([ref[:, j * HD:(j + 1) * HD], ref[:, 256 + j * HD:256 + (j + 1) * HD]], axis=1)
                left = left + jnp.dot(pick_left, both, preferred_element_type=F32)
        left = left.astype(BF)
        for core in range(2):
            send[at, core, :, 768:896] = left[:, core * HD:(core + 1) * HD].reshape(16, 16, HD)

    def start(k):
        copy = pltpu.make_async_remote_copy(
            src_ref=send.at[k // 2, (c + k % 2) % 2], dst_ref=recv.at[k],
            send_sem=send_sem.at[k], recv_sem=recv_sem.at[k],
            device_id=peer(k), device_id_type=MESH)
        copy.start()
        copies[k] = copy

    order = (4, 3, 5, 2, 6, 1, 7, 0)
    build(1)
    pl.semaphore_wait(barrier, 63)
    for rz in (4, 5, 6, 7):
        for i in range(8):
            start(rz * 8 + i)
    build(0)
    for rz in (3, 2, 1, 0):
        for i in range(8):
            if rz * 8 + i > 0:
                start(rz * 8 + i)
    recv[0] = send[0, c]

    lens = jnp.broadcast_to(len_ref[...], (16, HD))
    earlier = (iota((HD, HD), 0) < iota((HD, HD), 1)).astype(BF)
    starts = (
        jnp.dot((lens >> 8).astype(F32).astype(BF), earlier, preferred_element_type=F32) * 256.0
        + jnp.dot((lens & 255).astype(F32).astype(BF), earlier, preferred_element_type=F32))[0:1]
    starts = starts - ((me // 2) * CHIP).astype(F32)

    def mask(i, carry):
        row = (iota((256, HD), 0) + i * 256).astype(F32)
        first = jnp.max(jnp.where(starts <= row, starts, -1e9), axis=1, keepdims=True)
        rows = (iota((256, CHIP), 0) + i * 256).astype(F32)
        cols = iota((256, CHIP), 1).astype(F32)
        bias[pl.ds(i * 256, 256), :] = jnp.where((cols <= rows) & (cols >= first), 0.0, NEG)
        return carry

    lax.fori_loop(0, 3, mask, 0)

    block = (iota((HD, HD), 0) & 15) >> 1
    groups = ((4, 5), (6, 7), (3, 2), (1, 0))
    for step, pair in enumerate(groups):
        places = []
        for g, rz in enumerate(pair):
            for i in range(8):
                if rz * 8 + i > 0:
                    copies[rz * 8 + i].wait_recv()
            tail = recv[rz * 8:(rz + 1) * 8, :, 768:896]
            total = jnp.sum(tail.astype(F32), axis=0)
            places.append(total[12:13] * 16.0 + total[13:14] - 16.0)
            places.append(total[14:15] * 16.0 + total[15:16] - 16.0)
            dense[g * 256:g * 256 + HD, :] = recv[rz * 8:(rz + 1) * 8, :, 0:768].reshape(HD, 768)
            tail = tail.reshape(HD, HD)
            for b in range(6):
                dense[g * 256 + HD:(g + 1) * 256, b * HD:(b + 1) * HD] = jnp.where(block == b, tail, jnp.zeros_like(tail))
        places = jnp.concatenate(places, axis=1).astype(I32)

        def deliver(i, carry, step=step, places=places):
            at = pl.ds(i * 256, 256)
            pick = (iota((256, 512), 0) + i * 256 == places).astype(F32).astype(BF)
            got = jnp.dot(pick, dense[...], preferred_element_type=F32).astype(BF)
            placed[at, :] = got if step == 0 else placed[at, :] + got
            return carry

        lax.fori_loop(0, 3, deliver, 0)

    scale = 1.0 / math.sqrt(HD)
    swaps = []
    for j in range(2):
        for i in range(3):
            upto = (i + 1) * 256
            at = slice(i * 256, upto)
            scores = lax.dot_general(
                placed[at, j * HD:(j + 1) * HD], placed[0:upto, 256 + j * HD:256 + (j + 1) * HD],
                NT, preferred_element_type=F32) * scale + bias[at, 0:upto]
            top = jnp.max(scores, axis=1, keepdims=True)
            weights = jnp.exp(scores - top)
            total = jnp.sum(weights, axis=1, keepdims=True)
            mix = jnp.dot(weights.astype(BF), placed[0:upto, 512 + j * HD:512 + (j + 1) * HD], preferred_element_type=F32)
            mixed[at, j * HD:(j + 1) * HD] = (mix / total).astype(BF)
        cols = pl.ds(pl.multiple_of(c * 256 + j * HD, HD), HD)
        swap = pltpu.make_async_remote_copy(
            src_ref=mixed.at[pl.ds(pl.multiple_of((1 - c) * ROWS, ROWS), ROWS), j * HD:(j + 1) * HD],
            dst_ref=out_ref.at[:, cols],
            send_sem=swap_send.at[j], recv_sem=swap_recv.at[j],
            device_id=peer(1), device_id_type=MESH)
        swap.start()
        swaps.append(swap)
        out_ref[:, cols] = mixed[pl.ds(pl.multiple_of(c * ROWS, ROWS), ROWS), j * HD:(j + 1) * HD]
    for copy in copies.values():
        copy.wait_send()
    for swap in swaps:
        swap.wait()


def body(queries, keys, values, target_row, doc_lengths):
    vmem = pl.BlockSpec(memory_space=pltpu.VMEM)
    return pl.pallas_call(
        kernel,
        out_shape=jax.ShapeDtypeStruct(queries.shape, BF),
        in_specs=[vmem] * 5,
        out_specs=vmem,
        scratch_shapes=[
            pltpu.VMEM((32, 2, 16, WIDE), BF),
            pltpu.VMEM((64, 16, WIDE), BF),
            pltpu.VMEM((CHIP, 768), BF),
            pltpu.VMEM((CHIP, CHIP), F32),
            pltpu.VMEM((512, 768), BF),
            pltpu.VMEM((CHIP, 256), BF),
            pltpu.SemaphoreType.DMA((64,)),
            pltpu.SemaphoreType.DMA((64,)),
            pltpu.SemaphoreType.DMA((2,)),
            pltpu.SemaphoreType.DMA((2,)),
        ],
        compiler_params=pltpu.CompilerParams(collective_id=0, has_side_effects=True, vmem_limit_bytes=40 * 2**20),
    )(queries, keys, values, target_row.reshape(1, -1), doc_lengths.reshape(1, -1))


def solution(mesh):
    in_specs = (P("seq", "head"), P("seq", "head"), P("seq", "head"), P("seq"), P())
    return jax.shard_map(body, mesh=mesh, in_specs=in_specs, out_specs=P("seq", "head"), check_vma=False)
```

```python
import functools
import math

import jax
import jax.numpy as jnp
from jax import lax
from jax.experimental import pallas as pl
from jax.experimental.pallas import tpu as pltpu
from jax.sharding import PartitionSpec as P

HD = 128
ROWS = 384
CAP = 9
CHIP = 2 * ROWS
NZ, NX = 8, 4
NEG = -1e30
MESH = pl.DeviceIdType.MESH
BF = jnp.bfloat16
F32 = jnp.float32
I32 = jnp.int32
WIDE = 7 * HD
SELF = 56
Z_ORDER = (4, 3, 5, 2, 6, 1, 7, 0)
NT = (((1,), (1,)), ((), ()))


def iota(shape, dim):
    return lax.broadcasted_iota(I32, shape, dim)


def kernel(q_hbm, k_hbm, v_hbm, t_hbm, len_hbm, out_ref, q_ref, k_ref, v_ref, t_ref, len_ref, in_sem, send, recv, placed, bias, dense, mixed, send_sem, recv_sem, swap_send, swap_recv):
    me = lax.axis_index("seq")
    head = lax.axis_index("head")
    z, x, c = me // 8, (me // 2) % 4, me % 2

    def peer(k):
        rz, rx, xc = Z_ORDER[k // 8], (k // 2) % 4, k % 2
        return (((z + rz) % 8) * 8 + ((x + rx) % 4) * 2 + (c + xc) % 2, head)

    pairs = ((t_hbm, t_ref), (q_hbm, q_ref), (k_hbm, k_ref), (v_hbm, v_ref), (len_hbm, len_ref))
    fetch = [pltpu.make_async_copy(src, dst, in_sem.at[i]) for i, (src, dst) in enumerate(pairs)]
    for copy in fetch:
        copy.start()

    barrier = pltpu.get_barrier_semaphore()
    for k in range(64):
        if k == SELF:
            continue
        pl.semaphore_signal(barrier, inc=1, device_id=peer(k), device_id_type=MESH)

    fetch[0].wait()
    t = t_ref[...].reshape(1, ROWS)
    dev = jnp.floor((t.astype(F32) + 0.5) * (1.0 / ROWS)).astype(I32)
    local = t - dev * ROWS
    away = 4 - (((dev >> 3) - z) & 7)
    rzv = jnp.where(away > 0, 2 * away - 1, -2 * away)
    rxv = (((dev >> 1) & 3) - x) & 3
    cc = dev & 1
    m = rzv * 4 + rxv
    flags = iota((64, ROWS), 0) == m * 2 + cc
    before = (iota((ROWS, ROWS), 0) < iota((ROWS, ROWS), 1)).astype(BF)
    cum = jnp.dot(flags.astype(F32).astype(BF), before, preferred_element_type=F32)
    rank = jnp.sum(jnp.where(flags, cum, 0.0), axis=0, keepdims=True).astype(I32)
    s = cc * CAP + rank
    place = cc * ROWS + local
    hi, lo = ((place >> 4) + 1).astype(F32), (place & 15).astype(F32)
    over = s >= 16
    main_row = jnp.where(over, -1, m * 16 + s)
    left_row = jnp.where(over, m * 16 + s - 16, -1000)
    place_row = m * 16 + jnp.where(over, 14, 12)
    lanes = iota((HD, ROWS), 0)
    hot = []
    for core in range(2):
        kk = rxv * 2 + ((c + core) & 1)
        main_hot = lanes == kk * 16 + s
        left_hot = ((lanes >> 4) == kk) & ((lanes & 15) < 12) & ((lanes & 1) == s - 16)
        hot.append(jnp.where(over, left_hot.astype(F32), main_hot.astype(F32)).astype(BF))
    hot = jnp.concatenate(hot, axis=0)

    for copy in fetch[1:]:
        copy.wait()
    copies = {}

    def build(chunk):
        rows = iota((256, ROWS), 0) + chunk * 256
        pick = (rows == main_row).astype(F32).astype(BF)
        at = pl.ds(chunk * 16, 16)
        left = lax.dot_general(
            (jnp.where(rows == place_row, hi, 0.0) + jnp.where(rows == place_row + 1, lo, 0.0)).astype(BF),
            hot, NT, preferred_element_type=F32)
        for a, ref in enumerate((q_ref, k_ref, v_ref)):
            got = jnp.dot(pick, ref[...], preferred_element_type=F32).astype(BF)
            for core in range(2):
                send[at, core, :, a * 256:(a + 1) * 256] = got[:, core * 256:(core + 1) * 256].reshape(16, 16, 256)
            for j in range(2):
                b = a * 2 + j
                pick_left = (rows - 2 * b == left_row).astype(F32).astype(BF)
                both = jnp.concatenate([ref[:, j * HD:(j + 1) * HD], ref[:, 256 + j * HD:256 + (j + 1) * HD]], axis=1)
                left = left + jnp.dot(pick_left, both, preferred_element_type=F32)
        left = left.astype(BF)
        for core in range(2):
            send[at, core, :, 768:896] = left[:, core * HD:(core + 1) * HD].reshape(16, 16, HD)

    def start(k):
        copy = pltpu.make_async_remote_copy(
            src_ref=send.at[k // 2, (c + k % 2) % 2], dst_ref=recv.at[k],
            send_sem=send_sem.at[k], recv_sem=recv_sem.at[k],
            device_id=peer(k), device_id_type=MESH)
        copy.start()
        copies[k] = copy

    build(0)
    pl.semaphore_wait(barrier, 63)
    for k in range(32):
        start(k)
    build(1)
    for k in range(32, 64):
        if k != SELF:
            start(k)
    recv[SELF] = send[SELF // 2, c]

    lens = jnp.broadcast_to(len_ref[...].reshape(1, HD), (16, HD))
    earlier = (iota((HD, HD), 0) < iota((HD, HD), 1)).astype(BF)
    starts = (
        jnp.dot((lens >> 8).astype(F32).astype(BF), earlier, preferred_element_type=F32) * 256.0
        + jnp.dot((lens & 255).astype(F32).astype(BF), earlier, preferred_element_type=F32))[0:1]
    starts = starts - ((me // 2) * CHIP).astype(F32)

    def mask(i, carry):
        row = (iota((256, HD), 0) + i * 256).astype(F32)
        first = jnp.max(jnp.where(starts <= row, starts, -1e9), axis=1, keepdims=True)
        rows = (iota((256, CHIP), 0) + i * 256).astype(F32)
        cols = iota((256, CHIP), 1).astype(F32)
        bias[pl.ds(i * 256, 256), :] = jnp.where((cols <= rows) & (cols >= first), 0.0, NEG)
        return carry

    lax.fori_loop(0, 3, mask, 0)

    block = (iota((HD, HD), 0) & 15) >> 1
    groups = ((0, 1), (2, 3), (4, 5), (6, 7))
    for step, pair in enumerate(groups):
        places = []
        for g, rz in enumerate(pair):
            for i in range(8):
                if rz * 8 + i != SELF:
                    copies[rz * 8 + i].wait_recv()
            tail = recv[rz * 8:(rz + 1) * 8, :, 768:896]
            total = jnp.sum(tail.astype(F32), axis=0)
            places.append(total[12:13] * 16.0 + total[13:14] - 16.0)
            places.append(total[14:15] * 16.0 + total[15:16] - 16.0)
            dense[g * 256:g * 256 + HD, :] = recv[rz * 8:(rz + 1) * 8, :, 0:768].reshape(HD, 768)
            tail = tail.reshape(HD, HD)
            for b in range(6):
                dense[g * 256 + HD:(g + 1) * 256, b * HD:(b + 1) * HD] = jnp.where(block == b, tail, jnp.zeros_like(tail))
        places = jnp.concatenate(places, axis=1).astype(I32)

        def deliver(i, carry, step=step, places=places):
            at = pl.ds(i * 256, 256)
            pick = (iota((256, 512), 0) + i * 256 == places).astype(F32).astype(BF)
            got = jnp.dot(pick, dense[...], preferred_element_type=F32).astype(BF)
            placed[at, :] = got if step == 0 else placed[at, :] + got
            return carry

        lax.fori_loop(0, 3, deliver, 0)

    scale = 1.0 / math.sqrt(HD)
    swaps = []
    for j in range(2):
        for i in range(3):
            upto = (i + 1) * 256
            at = slice(i * 256, upto)
            scores = lax.dot_general(
                placed[at, j * HD:(j + 1) * HD], placed[0:upto, 256 + j * HD:256 + (j + 1) * HD],
                NT, preferred_element_type=F32) * scale + bias[at, 0:upto]
            top = jnp.max(scores, axis=1, keepdims=True)
            weights = jnp.exp(scores - top)
            total = jnp.sum(weights, axis=1, keepdims=True)
            mix = jnp.dot(weights.astype(BF), placed[0:upto, 512 + j * HD:512 + (j + 1) * HD], preferred_element_type=F32)
            mixed[at, j * HD:(j + 1) * HD] = (mix / total).astype(BF)
        cols = pl.ds(pl.multiple_of(c * 256 + j * HD, HD), HD)
        swap = pltpu.make_async_remote_copy(
            src_ref=mixed.at[pl.ds(pl.multiple_of((1 - c) * ROWS, ROWS), ROWS), j * HD:(j + 1) * HD],
            dst_ref=out_ref.at[:, cols],
            send_sem=swap_send.at[j], recv_sem=swap_recv.at[j],
            device_id=peer(SELF + 1), device_id_type=MESH)
        swap.start()
        swaps.append(swap)
        out_ref[:, cols] = mixed[pl.ds(pl.multiple_of(c * ROWS, ROWS), ROWS), j * HD:(j + 1) * HD]
    for copy in copies.values():
        copy.wait_send()
    for swap in swaps:
        swap.wait()


def body(queries, keys, values, target_row, doc_lengths):
    vmem = pl.BlockSpec(memory_space=pltpu.VMEM)
    return pl.pallas_call(
        kernel,
        out_shape=jax.ShapeDtypeStruct(queries.shape, BF),
        in_specs=[pl.BlockSpec(memory_space=pl.ANY)] * 5,
        out_specs=vmem,
        scratch_shapes=[
            pltpu.VMEM(queries.shape, BF),
            pltpu.VMEM(queries.shape, BF),
            pltpu.VMEM(queries.shape, BF),
            pltpu.VMEM((ROWS,), I32),
            pltpu.VMEM((HD,), I32),
            pltpu.SemaphoreType.DMA((5,)),
            pltpu.VMEM((32, 2, 16, WIDE), BF),
            pltpu.VMEM((64, 16, WIDE), BF),
            pltpu.VMEM((CHIP, 768), BF),
            pltpu.VMEM((CHIP, CHIP), F32),
            pltpu.VMEM((512, 768), BF),
            pltpu.VMEM((CHIP, 256), BF),
            pltpu.SemaphoreType.DMA((64,)),
            pltpu.SemaphoreType.DMA((64,)),
            pltpu.SemaphoreType.DMA((2,)),
            pltpu.SemaphoreType.DMA((2,)),
        ],
        compiler_params=pltpu.CompilerParams(collective_id=0, has_side_effects=True, vmem_limit_bytes=535 * 2**20 // 10),
    )(queries, keys, values, target_row, doc_lengths)


def solution(mesh):
    in_specs = (P("seq", "head"), P("seq", "head"), P("seq", "head"), P("seq"), P())
    return jax.shard_map(body, mesh=mesh, in_specs=in_specs, out_specs=P("seq", "head"), check_vma=False)
```

```python
import functools
import math

import jax
import jax.numpy as jnp
from jax import lax
from jax.experimental import pallas as pl
from jax.experimental.pallas import tpu as pltpu
from jax.sharding import PartitionSpec as P

HD = 128
ROWS = 384
CAP = 9
CHIP = 2 * ROWS
NZ, NX = 8, 4
NEG = -1e30
MESH = pl.DeviceIdType.MESH
BF = jnp.bfloat16
F32 = jnp.float32
I32 = jnp.int32
WIDE = 7 * HD


def spread(zs, first=0, last=8):
    return [(zz, i) for i in range(first, last) for zz in zs]


def mixed_with(a, b):
    short, long = sorted((a, b), key=len)
    out = []
    for n, each in enumerate(long):
        out.append(each)
        out += short[n * len(short) // len(long):(n + 1) * len(short) // len(long)]
    return out


LOW_SENDS = ([(zz, i) for zz in range(4) for i in range(8)], [(zz, i) for zz in range(4,8) for i in range(8)])
HIGH_SENDS = (spread((0, 3, 1, 2), 0, 2), mixed_with(spread((0, 3, 1, 2), 2), spread((4, 7, 5, 6))))
NT = (((1,), (1,)), ((), ()))


def iota(shape, dim):
    return lax.broadcasted_iota(I32, shape, dim)


def kernel(q_hbm, k_hbm, v_hbm, t_ref, len_ref, out_ref, q_ref, k_ref, v_ref, in_sem, send, recv, placed, bias, dense, mixed, ready, send_sem, recv_sem, swap_send, swap_recv):
    me = lax.axis_index("seq")
    head = lax.axis_index("head")
    z, x, c = me // 8, (me // 2) % 4, me % 2

    def device(zz, i):
        return (zz * 8 + ((x + i // 2) % 4) * 2 + (c + i % 2) % 2, head)

    pairs = ((q_hbm, q_ref), (k_hbm, k_ref), (v_hbm, v_ref))
    fetch = [pltpu.make_async_copy(src, dst, in_sem.at[i]) for i, (src, dst) in enumerate(pairs)]
    for copy in fetch:
        copy.start()

    barrier = pltpu.get_barrier_semaphore()
    for i in range(1, 8):
        pl.semaphore_signal(barrier, inc=1, device_id=device(z, i), device_id_type=MESH)
    for zz in range(1, 8):

        @pl.when(zz > z)
        def _(zz=zz):
            for i in range(8):
                pl.semaphore_signal(barrier, inc=1, device_id=device(zz, i), device_id_type=MESH)

    pl.semaphore_wait(barrier, z * 8 + 7)
    for zz in range(7):

        @pl.when(zz < z)
        def _(zz=zz):
            for i in range(8):
                pl.semaphore_signal(ready.at[z], inc=1, device_id=device(zz, i), device_id_type=MESH)

    t = t_ref[...]
    dev = jnp.floor((t.astype(F32) + 0.5) * (1.0 / ROWS)).astype(I32)
    local = t - dev * ROWS
    rxv = (((dev >> 1) & 3) - x) & 3
    cc = dev & 1
    m = (dev >> 3) * 4 + rxv
    flags = iota((64, ROWS), 0) == m * 2 + cc
    before = (iota((ROWS, ROWS), 0) < iota((ROWS, ROWS), 1)).astype(BF)
    cum = jnp.dot(flags.astype(F32).astype(BF), before, preferred_element_type=F32)
    rank = jnp.sum(jnp.where(flags, cum, 0.0), axis=0, keepdims=True).astype(I32)
    s = cc * CAP + rank
    place = cc * ROWS + local
    hi, lo = ((place >> 4) + 1).astype(F32), (place & 15).astype(F32)
    over = s >= 16
    main_row = jnp.where(over, -1, m * 16 + s)
    left_row = jnp.where(over, m * 16 + s - 16, -1000)
    place_row = m * 16 + jnp.where(over, 14, 12)
    lanes = iota((HD, ROWS), 0)
    hot = []
    for core in range(2):
        kk = rxv * 2 + ((c + core) & 1)
        main_hot = lanes == kk * 16 + s
        left_hot = ((lanes >> 4) == kk) & ((lanes & 15) < 12) & ((lanes & 1) == s - 16)
        hot.append(jnp.where(over, left_hot.astype(F32), main_hot.astype(F32)).astype(BF))
    hot = jnp.concatenate(hot, axis=0)

    for copy in fetch:
        copy.wait()

    def build(chunk):
        rows = iota((256, ROWS), 0) + chunk * 256
        pick = (rows == main_row).astype(F32).astype(BF)
        at = pl.ds(chunk * 16, 16)
        left = lax.dot_general(
            (jnp.where(rows == place_row, hi, 0.0) + jnp.where(rows == place_row + 1, lo, 0.0)).astype(BF),
            hot, NT, preferred_element_type=F32)
        for a, ref in enumerate((q_ref, k_ref, v_ref)):
            got = jnp.dot(pick, ref[...], preferred_element_type=F32).astype(BF)
            for core in range(2):
                send[at, core, :, a * 256:(a + 1) * 256] = got[:, core * 256:(core + 1) * 256].reshape(16, 16, 256)
            for j in range(2):
                b = a * 2 + j
                pick_left = (rows - 2 * b == left_row).astype(F32).astype(BF)
                both = jnp.concatenate([ref[:, j * HD:(j + 1) * HD], ref[:, 256 + j * HD:256 + (j + 1) * HD]], axis=1)
                left = left + jnp.dot(pick_left, both, preferred_element_type=F32)
        left = left.astype(BF)
        for core in range(2):
            send[at, core, :, 768:896] = left[:, core * HD:(core + 1) * HD].reshape(16, 16, HD)

    def copy_of(zz, i, slot):
        return pltpu.make_async_remote_copy(
            src_ref=send.at[zz * 4 + i // 2, (c + i % 2) % 2], dst_ref=recv.at[slot],
            send_sem=send_sem.at[zz * 8 + i], recv_sem=recv_sem.at[slot],
            device_id=device(zz, i), device_id_type=MESH)

    def start(sends, greeted):
        for zz, i in sends:
            if zz > 0 and zz not in greeted:
                greeted.add(zz)

                @pl.when(zz > z)
                def _(zz=zz):
                    pl.semaphore_wait(ready.at[zz], 8)

            if i > 0:
                copy_of(zz, i, z * 8 + i).start()
            else:

                @pl.when(zz != z)
                def _(zz=zz):
                    copy_of(zz, 0, z * 8).start()

    def send_part(part):
        for near, sends in enumerate((LOW_SENDS, HIGH_SENDS)):

            @pl.when((z >= 4) == (near == 1))
            def _(near=near, sends=sends):
                start(sends[part], met[near])

    met = (set(), set())

    build(0)
    send_part(0)
    build(1)
    send_part(1)
    recv[z * 8] = send[z * 4, c]

    lens = jnp.broadcast_to(len_ref[...], (16, HD))
    earlier = (iota((HD, HD), 0) < iota((HD, HD), 1)).astype(BF)
    starts = (
        jnp.dot((lens >> 8).astype(F32).astype(BF), earlier, preferred_element_type=F32) * 256.0
        + jnp.dot((lens & 255).astype(F32).astype(BF), earlier, preferred_element_type=F32))[0:1]
    starts = starts - ((me // 2) * CHIP).astype(F32)

    def mask(i, carry):
        row = (iota((256, HD), 0) + i * 256).astype(F32)
        first = jnp.max(jnp.where(starts <= row, starts, -1e9), axis=1, keepdims=True)
        rows = (iota((256, CHIP), 0) + i * 256).astype(F32)
        cols = iota((256, CHIP), 1).astype(F32)
        bias[pl.ds(i * 256, 256), :] = jnp.where((cols <= rows) & (cols >= first), 0.0, NEG)
        return carry

    lax.fori_loop(0, 3, mask, 0)

    block = (iota((HD, HD), 0) & 15) >> 1
    groups = ((0, 1), (2, 3), (4, 5), (6, 7))
    for step, pair in enumerate(groups):
        places = []
        for g, rz in enumerate(pair):
            @pl.when(rz != z)
            def _(rz=rz):
                copy_of(rz, 0, rz * 8).wait_recv()

            for i in range(1, 8):
                copy_of(rz, i, rz * 8 + i).wait_recv()
            tail = recv[rz * 8:(rz + 1) * 8, :, 768:896]
            total = jnp.sum(tail.astype(F32), axis=0)
            places.append(total[12:13] * 16.0 + total[13:14] - 16.0)
            places.append(total[14:15] * 16.0 + total[15:16] - 16.0)
            dense[g * 256:g * 256 + HD, :] = recv[rz * 8:(rz + 1) * 8, :, 0:768].reshape(HD, 768)
            tail = tail.reshape(HD, HD)
            for b in range(6):
                dense[g * 256 + HD:(g + 1) * 256, b * HD:(b + 1) * HD] = jnp.where(block == b, tail, jnp.zeros_like(tail))
        places = jnp.concatenate(places, axis=1).astype(I32)

        def deliver(i, carry, step=step, places=places):
            at = pl.ds(i * 256, 256)
            pick = (iota((256, 512), 0) + i * 256 == places).astype(F32).astype(BF)
            got = jnp.dot(pick, dense[...], preferred_element_type=F32).astype(BF)
            placed[at, :] = got if step == 0 else placed[at, :] + got
            return carry

        lax.fori_loop(0, 3, deliver, 0)

    scale = 1.0 / math.sqrt(HD)
    swaps = []
    for j in range(2):
        for i in range(3):
            upto = (i + 1) * 256
            at = slice(i * 256, upto)
            scores = lax.dot_general(
                placed[at, j * HD:(j + 1) * HD], placed[0:upto, 256 + j * HD:256 + (j + 1) * HD],
                NT, preferred_element_type=F32) * scale + bias[at, 0:upto]
            top = jnp.max(scores, axis=1, keepdims=True)
            weights = jnp.exp(scores - top)
            total = jnp.sum(weights, axis=1, keepdims=True)
            mix = jnp.dot(weights.astype(BF), placed[0:upto, 512 + j * HD:512 + (j + 1) * HD], preferred_element_type=F32)
            mixed[at, j * HD:(j + 1) * HD] = (mix / total).astype(BF)
        cols = pl.ds(pl.multiple_of(c * 256 + j * HD, HD), HD)
        swap = pltpu.make_async_remote_copy(
            src_ref=mixed.at[pl.ds(pl.multiple_of((1 - c) * ROWS, ROWS), ROWS), j * HD:(j + 1) * HD],
            dst_ref=out_ref.at[:, cols],
            send_sem=swap_send.at[j], recv_sem=swap_recv.at[j],
            device_id=device(z, 1), device_id_type=MESH)
        swap.start()
        swaps.append(swap)
        out_ref[:, cols] = mixed[pl.ds(pl.multiple_of(c * ROWS, ROWS), ROWS), j * HD:(j + 1) * HD]
    for zz in range(8):

        @pl.when(zz != z)
        def _(zz=zz):
            copy_of(zz, 0, z * 8).wait_send()

        for i in range(1, 8):
            copy_of(zz, i, z * 8 + i).wait_send()
    for swap in swaps:
        swap.wait()


def body(queries, keys, values, target_row, doc_lengths):
    vmem = pl.BlockSpec(memory_space=pltpu.VMEM)
    return pl.pallas_call(
        kernel,
        out_shape=jax.ShapeDtypeStruct(queries.shape, BF),
        in_specs=[pl.BlockSpec(memory_space=pl.ANY)] * 3 + [vmem] * 2,
        out_specs=vmem,
        scratch_shapes=[
            pltpu.VMEM(queries.shape, BF),
            pltpu.VMEM(queries.shape, BF),
            pltpu.VMEM(queries.shape, BF),
            pltpu.SemaphoreType.DMA((3,)),
            pltpu.VMEM((32, 2, 16, WIDE), BF),
            pltpu.VMEM((64, 16, WIDE), BF),
            pltpu.VMEM((CHIP, 768), BF),
            pltpu.VMEM((CHIP, CHIP), F32),
            pltpu.VMEM((512, 768), BF),
            pltpu.VMEM((CHIP, 256), BF),
            pltpu.SemaphoreType.REGULAR((8,)),
            pltpu.SemaphoreType.DMA((64,)),
            pltpu.SemaphoreType.DMA((64,)),
            pltpu.SemaphoreType.DMA((2,)),
            pltpu.SemaphoreType.DMA((2,)),
        ],
        compiler_params=pltpu.CompilerParams(collective_id=0, has_side_effects=True, vmem_limit_bytes=535 * 2**20 // 10),
    )(queries, keys, values, target_row.reshape(1, -1), doc_lengths.reshape(1, -1))


def solution(mesh):
    in_specs = (P("seq", "head"), P("seq", "head"), P("seq", "head"), P("seq"), P())
    return jax.shard_map(body, mesh=mesh, in_specs=in_specs, out_specs=P("seq", "head"), check_vma=False)
```

```python
import functools
import math

import jax
import jax.numpy as jnp
from jax import lax
from jax.experimental import pallas as pl
from jax.experimental.pallas import tpu as pltpu
from jax.sharding import PartitionSpec as P

HD = 128
ROWS = 384
CAP = 9
CHIP = 2 * ROWS
NZ, NX = 8, 4
NEG = -1e30
MESH = pl.DeviceIdType.MESH
BF = jnp.bfloat16
F32 = jnp.float32
I32 = jnp.int32
WIDE = 7 * HD


def spread(zs, first=0, last=8):
    return [(zz, i) for i in range(first, last) for zz in zs]


def mixed_with(a, b):
    short, long = sorted((a, b), key=len)
    out = []
    for n, each in enumerate(long):
        out.append(each)
        out += short[n * len(short) // len(long):(n + 1) * len(short) // len(long)]
    return out


LOW_SENDS = ([(zz, i) for zz in range(4) for i in range(8)], [(zz, i) for zz in range(4,8) for i in range(8)])
HIGH_SENDS = (spread((0, 3, 1, 2), 0, 2), mixed_with(spread((0, 3, 1, 2), 2), spread((4, 7, 5, 6))))
NT = (((1,), (1,)), ((), ()))


def iota(shape, dim):
    return lax.broadcasted_iota(I32, shape, dim)


def kernel(q_hbm, k_hbm, v_hbm, t_ref, len_ref, out_ref, q_ref, k_ref, v_ref, in_sem, send, recv, placed, bias, dense, mixed, ready, send_sem, recv_sem, swap_send, swap_recv):
    me = lax.axis_index("seq")
    head = lax.axis_index("head")
    z, x, c = me // 8, (me // 2) % 4, me % 2

    def device(zz, i):
        return (zz * 8 + ((x + i // 2) % 4) * 2 + (c + i % 2) % 2, head)

    pairs = ((q_hbm, q_ref), (k_hbm, k_ref), (v_hbm, v_ref))
    fetch = [pltpu.make_async_copy(src, dst, in_sem.at[i]) for i, (src, dst) in enumerate(pairs)]
    for copy in fetch:
        copy.start()

    barrier = pltpu.get_barrier_semaphore()
    for i in range(1, 8):
        pl.semaphore_signal(barrier, inc=1, device_id=device(z, i), device_id_type=MESH)
    for zz in range(1, 8):

        @pl.when(zz > z)
        def _(zz=zz):
            for i in range(8):
                pl.semaphore_signal(barrier, inc=1, device_id=device(zz, i), device_id_type=MESH)

    t = t_ref[...]
    dev = jnp.floor((t.astype(F32) + 0.5) * (1.0 / ROWS)).astype(I32)
    local = t - dev * ROWS
    rxv = (((dev >> 1) & 3) - x) & 3
    cc = dev & 1
    m = (dev >> 3) * 4 + rxv
    flags = iota((64, ROWS), 0) == m * 2 + cc
    before = (iota((ROWS, ROWS), 0) < iota((ROWS, ROWS), 1)).astype(BF)
    cum = jnp.dot(flags.astype(F32).astype(BF), before, preferred_element_type=F32)
    rank = jnp.sum(jnp.where(flags, cum, 0.0), axis=0, keepdims=True).astype(I32)
    s = cc * CAP + rank
    place = cc * ROWS + local
    hi, lo = ((place >> 4) + 1).astype(F32), (place & 15).astype(F32)
    over = s >= 16
    main_row = jnp.where(over, -1, m * 16 + s)
    left_row = jnp.where(over, m * 16 + s - 16, -1000)
    place_row = m * 16 + jnp.where(over, 14, 12)
    pl.semaphore_wait(barrier, z * 8 + 7)
    for zz in range(7):

        @pl.when(zz < z)
        def _(zz=zz):
            pl.semaphore_signal(ready.at[z], inc=1, device_id=device(zz, 0), device_id_type=MESH)

    lanes = iota((HD, ROWS), 0)
    hot = []
    for core in range(2):
        kk = rxv * 2 + ((c + core) & 1)
        kk = (kk & 3) + 4 * (z % 2)
        main_hot = lanes == kk * 16 + s
        left_hot = ((lanes >> 4) == kk) & ((lanes & 15) < 12) & ((lanes & 1) == s - 16)
        hot.append(jnp.where(over, left_hot.astype(F32), main_hot.astype(F32)).astype(BF))
    hot = jnp.concatenate(hot, axis=0)

    for copy in fetch:
        copy.wait()

    def build(chunk):
        rows = iota((256, ROWS), 0) + chunk * 256
        pick = (rows == main_row).astype(F32).astype(BF)
        at = pl.ds(chunk * 16, 16)
        left = lax.dot_general(
            (jnp.where(rows == place_row, hi, 0.0) + jnp.where(rows == place_row + 1, lo, 0.0)).astype(BF),
            hot, NT, preferred_element_type=F32)
        for a, ref in enumerate((q_ref, k_ref, v_ref)):
            got = jnp.dot(pick, ref[...], preferred_element_type=F32).astype(BF)
            for core in range(2):
                send[at, core, :, a * 256:(a + 1) * 256] = got[:, core * 256:(core + 1) * 256].reshape(16, 16, 256)
            for j in range(2):
                b = a * 2 + j
                pick_left = (rows - 2 * b == left_row).astype(F32).astype(BF)
                both = jnp.concatenate([ref[:, j * HD:(j + 1) * HD], ref[:, 256 + j * HD:256 + (j + 1) * HD]], axis=1)
                left = left + jnp.dot(pick_left, both, preferred_element_type=F32)
        left = left.astype(BF)
        for core in range(2):
            send[at, core, :, 768:896] = left[:, core * HD:(core + 1) * HD].reshape(16, 16, HD)

    def copy_of(zz, i, slot):
        return pltpu.make_async_remote_copy(
            src_ref=send.at[zz * 4 + i // 2, (c + i % 2) % 2], dst_ref=recv.at[slot],
            send_sem=send_sem.at[zz * 8 + i], recv_sem=recv_sem.at[slot],
            device_id=device(zz, i), device_id_type=MESH)

    def start(sends, greeted):
        for zz, i in sends:
            if zz > 0 and zz not in greeted:
                greeted.add(zz)

                @pl.when(zz > z)
                def _(zz=zz):
                    pl.semaphore_wait(ready.at[zz], 1)

            if i > 0:
                copy_of(zz, i, z * 8 + i).start()
            else:

                @pl.when(zz != z)
                def _(zz=zz):
                    copy_of(zz, 0, z * 8).start()

    def send_part(part):
        for near, sends in enumerate((LOW_SENDS, HIGH_SENDS)):

            @pl.when((z >= 4) == (near == 1))
            def _(near=near, sends=sends):
                start(sends[part], met[near])

    met = (set(), set())

    build(0)
    send_part(0)
    build(1)
    send_part(1)
    recv[z * 8] = send[z * 4, c]

    lens = jnp.broadcast_to(len_ref[...], (16, HD))
    earlier = (iota((HD, HD), 0) < iota((HD, HD), 1)).astype(BF)
    starts = (
        jnp.dot((lens >> 8).astype(F32).astype(BF), earlier, preferred_element_type=F32) * 256.0
        + jnp.dot((lens & 255).astype(F32).astype(BF), earlier, preferred_element_type=F32))[0:1]
    starts = starts - ((me // 2) * CHIP).astype(F32)

    def mask(i, carry):
        row = (iota((256, HD), 0) + i * 256).astype(F32)
        first = jnp.max(jnp.where(starts <= row, starts, -1e9), axis=1, keepdims=True)
        rows = (iota((256, CHIP), 0) + i * 256).astype(F32)
        cols = iota((256, CHIP), 1).astype(F32)
        bias[pl.ds(i * 256, 256), :] = jnp.where((cols <= rows) & (cols >= first), 0.0, NEG)
        return carry

    lax.fori_loop(0, 3, mask, 0)

    block = (iota((64, HD), 0) & 15) >> 1
    for step in range(4):
        places = []
        for g in range(2):
            total = None
            for odd in range(2):
                zz = step // 2 * 4 + g * 2 + odd
                first = zz * 8 + step % 2 * 4
                for i in range(step % 2 * 4, step % 2 * 4 + 4):
                    if i > 0:
                        copy_of(zz, i, zz * 8 + i).wait_recv()
                    else:

                        @pl.when(zz != z)
                        def _(zz=zz):
                            copy_of(zz, 0, zz * 8).wait_recv()

                at = slice(g * 256 + odd * 64, g * 256 + odd * 64 + 64)
                at_left = slice(g * 256 + HD + odd * 64, g * 256 + HD + odd * 64 + 64)
                tail = recv[first:first + 4, :, 768:896]
                part = jnp.sum(tail.astype(F32), axis=0)
                total = part if total is None else total + part
                dense[at, :] = recv[first:first + 4, :, 0:768].reshape(64, 768)
                tail = tail.reshape(64, HD)
                for b in range(6):
                    dense[at_left, b * HD:(b + 1) * HD] = jnp.where(block == b, tail, jnp.zeros_like(tail))
            places.append(total[12:13] * 16.0 + total[13:14] - 16.0)
            places.append(total[14:15] * 16.0 + total[15:16] - 16.0)
        places = jnp.concatenate(places, axis=1).astype(I32)

        def deliver(i, carry, step=step, places=places):
            at = pl.ds(i * 256, 256)
            pick = (iota((256, 512), 0) + i * 256 == places).astype(F32).astype(BF)
            got = jnp.dot(pick, dense[...], preferred_element_type=F32).astype(BF)
            placed[at, :] = got if step == 0 else placed[at, :] + got
            return carry

        lax.fori_loop(0, 3, deliver, 0)

    scale = 1.0 / math.sqrt(HD)
    swaps = []
    for j in range(2):
        for i in range(3):
            upto = (i + 1) * 256
            at = slice(i * 256, upto)
            scores = lax.dot_general(
                placed[at, j * HD:(j + 1) * HD], placed[0:upto, 256 + j * HD:256 + (j + 1) * HD],
                NT, preferred_element_type=F32) * scale + bias[at, 0:upto]
            top = jnp.max(scores, axis=1, keepdims=True)
            weights = jnp.exp(scores - top)
            total = jnp.sum(weights, axis=1, keepdims=True)
            mix = jnp.dot(weights.astype(BF), placed[0:upto, 512 + j * HD:512 + (j + 1) * HD], preferred_element_type=F32)
            mixed[at, j * HD:(j + 1) * HD] = (mix / total).astype(BF)
        cols = pl.ds(pl.multiple_of(c * 256 + j * HD, HD), HD)
        swap = pltpu.make_async_remote_copy(
            src_ref=mixed.at[pl.ds(pl.multiple_of((1 - c) * ROWS, ROWS), ROWS), j * HD:(j + 1) * HD],
            dst_ref=out_ref.at[:, cols],
            send_sem=swap_send.at[j], recv_sem=swap_recv.at[j],
            device_id=device(z, 1), device_id_type=MESH)
        swap.start()
        swaps.append(swap)
        out_ref[:, cols] = mixed[pl.ds(pl.multiple_of(c * ROWS, ROWS), ROWS), j * HD:(j + 1) * HD]
    for zz in range(8):

        @pl.when(zz != z)
        def _(zz=zz):
            copy_of(zz, 0, z * 8).wait_send()

        for i in range(1, 8):
            copy_of(zz, i, z * 8 + i).wait_send()
    for swap in swaps:
        swap.wait()


def body(queries, keys, values, target_row, doc_lengths):
    vmem = pl.BlockSpec(memory_space=pltpu.VMEM)
    return pl.pallas_call(
        kernel,
        out_shape=jax.ShapeDtypeStruct(queries.shape, BF),
        in_specs=[pl.BlockSpec(memory_space=pl.ANY)] * 3 + [vmem] * 2,
        out_specs=vmem,
        scratch_shapes=[
            pltpu.VMEM(queries.shape, BF),
            pltpu.VMEM(queries.shape, BF),
            pltpu.VMEM(queries.shape, BF),
            pltpu.SemaphoreType.DMA((3,)),
            pltpu.VMEM((32, 2, 16, WIDE), BF),
            pltpu.VMEM((64, 16, WIDE), BF),
            pltpu.VMEM((CHIP, 768), BF),
            pltpu.VMEM((CHIP, CHIP), F32),
            pltpu.VMEM((512, 768), BF),
            pltpu.VMEM((CHIP, 256), BF),
            pltpu.SemaphoreType.REGULAR((8,)),
            pltpu.SemaphoreType.DMA((64,)),
            pltpu.SemaphoreType.DMA((64,)),
            pltpu.SemaphoreType.DMA((2,)),
            pltpu.SemaphoreType.DMA((2,)),
        ],
        compiler_params=pltpu.CompilerParams(collective_id=0, has_side_effects=True, vmem_limit_bytes=535 * 2**20 // 10),
    )(queries, keys, values, target_row.reshape(1, -1), doc_lengths.reshape(1, -1))


def solution(mesh):
    in_specs = (P("seq", "head"), P("seq", "head"), P("seq", "head"), P("seq"), P())
    return jax.shard_map(body, mesh=mesh, in_specs=in_specs, out_specs=P("seq", "head"), check_vma=False)
```

```python
import functools
import math

import jax
import jax.numpy as jnp
from jax import lax
from jax.experimental import pallas as pl
from jax.experimental.pallas import tpu as pltpu
from jax.sharding import PartitionSpec as P

HD = 128
ROWS = 384
CAP = 9
CHIP = 2 * ROWS
NZ, NX = 8, 4
NEG = -1e30
MESH = pl.DeviceIdType.MESH
BF = jnp.bfloat16
F32 = jnp.float32
I32 = jnp.int32
WIDE = 7 * HD


def spread(zs, first=0, last=8):
    return [(zz, i) for i in range(first, last) for zz in zs]


def mixed_with(a, b):
    short, long = sorted((a, b), key=len)
    out = []
    for n, each in enumerate(long):
        out.append(each)
        out += short[n * len(short) // len(long):(n + 1) * len(short) // len(long)]
    return out


LOW_SENDS = ([(zz, i) for zz in range(4) for i in range(8)], [(zz, i) for zz in range(4,8) for i in range(8)])
HIGH_SENDS = (spread((0, 3, 1, 2), 0, 2), mixed_with(spread((0, 3, 1, 2), 2), spread((4, 7, 5, 6))))
NT = (((1,), (1,)), ((), ()))


def iota(shape, dim):
    return lax.broadcasted_iota(I32, shape, dim)


def kernel(q_hbm, k_hbm, v_hbm, t_ref, len_ref, out_ref, q_ref, k_ref, v_ref, in_sem, send, recv, placed, bias, dense, mixed, ready, send_sem, recv_sem, swap_send, swap_recv):
    me = lax.axis_index("seq")
    head = lax.axis_index("head")
    z, x, c = me // 8, (me // 2) % 4, me % 2

    def device(zz, i):
        return (zz * 8 + ((x + i // 2) % 4) * 2 + (c + i % 2) % 2, head)

    pairs = ((q_hbm, q_ref), (k_hbm, k_ref), (v_hbm, v_ref))
    fetch = [pltpu.make_async_copy(src, dst, in_sem.at[i]) for i, (src, dst) in enumerate(pairs)]
    for copy in fetch:
        copy.start()

    barrier = pltpu.get_barrier_semaphore()
    for i in range(1, 8):
        pl.semaphore_signal(barrier, inc=1, device_id=device(z, i), device_id_type=MESH)
    for zz in range(1, 8):

        @pl.when(zz > z)
        def _(zz=zz):
            for i in range(8):
                pl.semaphore_signal(barrier, inc=1, device_id=device(zz, i), device_id_type=MESH)

    t = t_ref[...]
    dev = jnp.floor((t.astype(F32) + 0.5) * (1.0 / ROWS)).astype(I32)
    local = t - dev * ROWS
    rxv = (((dev >> 1) & 3) - x) & 3
    cc = dev & 1
    m = (dev >> 3) * 4 + rxv
    flags = iota((64, ROWS), 0) == m * 2 + cc
    before = (iota((ROWS, ROWS), 0) < iota((ROWS, ROWS), 1)).astype(BF)
    cum = jnp.dot(flags.astype(F32).astype(BF), before, preferred_element_type=F32)
    rank = jnp.sum(jnp.where(flags, cum, 0.0), axis=0, keepdims=True).astype(I32)
    s = cc * CAP + rank
    place = cc * ROWS + local
    hi, lo = ((place >> 4) + 1).astype(F32), (place & 15).astype(F32)
    over = s >= 16
    main_row = jnp.where(over, -1, m * 16 + s)
    left_row = jnp.where(over, m * 16 + s - 16, -1000)
    place_row = m * 16 + jnp.where(over, 14, 12)
    pl.semaphore_wait(barrier, z * 8 + 7)
    for zz in range(7):

        @pl.when(zz < z)
        def _(zz=zz):
            pl.semaphore_signal(ready.at[z], inc=1, device_id=device(zz, 0), device_id_type=MESH)

    lanes = iota((HD, ROWS), 0)
    hot = []
    for core in range(2):
        kk = rxv * 2 + ((c + core) & 1)
        kk = (kk & 3) + 4 * (z % 2)
        main_hot = lanes == kk * 16 + s
        left_hot = ((lanes >> 4) == kk) & ((lanes & 15) < 12) & ((lanes & 1) == s - 16)
        hot.append(jnp.where(over, left_hot.astype(F32), main_hot.astype(F32)).astype(BF))
    hot = jnp.concatenate(hot, axis=0)

    for copy in fetch:
        copy.wait()

    def build(chunk):
        rows = iota((256, ROWS), 0) + chunk * 256
        pick = (rows == main_row).astype(F32).astype(BF)
        at = pl.ds(chunk * 16, 16)
        left = lax.dot_general(
            (jnp.where(rows == place_row, hi, 0.0) + jnp.where(rows == place_row + 1, lo, 0.0)).astype(BF),
            hot, NT, preferred_element_type=F32)
        for a, ref in enumerate((q_ref, k_ref, v_ref)):
            got = jnp.dot(pick, ref[...], preferred_element_type=F32).astype(BF)
            for core in range(2):
                send[at, core, :, a * 256:(a + 1) * 256] = got[:, core * 256:(core + 1) * 256].reshape(16, 16, 256)
            for j in range(2):
                b = a * 2 + j
                pick_left = (rows - 2 * b == left_row).astype(F32).astype(BF)
                both = jnp.concatenate([ref[:, j * HD:(j + 1) * HD], ref[:, 256 + j * HD:256 + (j + 1) * HD]], axis=1)
                left = left + jnp.dot(pick_left, both, preferred_element_type=F32)
        left = left.astype(BF)
        for core in range(2):
            send[at, core, :, 768:896] = left[:, core * HD:(core + 1) * HD].reshape(16, 16, HD)

    def copy_of(zz, i, slot):
        return pltpu.make_async_remote_copy(
            src_ref=send.at[zz * 4 + i // 2, (c + i % 2) % 2], dst_ref=recv.at[slot],
            send_sem=send_sem.at[zz * 8 + i], recv_sem=recv_sem.at[slot],
            device_id=device(zz, i), device_id_type=MESH)

    def start(sends, greeted):
        for zz, i in sends:
            if zz > 0 and zz not in greeted:
                greeted.add(zz)

                @pl.when(zz > z)
                def _(zz=zz):
                    pl.semaphore_wait(ready.at[zz], 1)

            if i > 0:
                copy_of(zz, i, z * 8 + i).start()
            else:

                @pl.when(zz != z)
                def _(zz=zz):
                    copy_of(zz, 0, z * 8).start()

    def send_part(part):
        for near, sends in enumerate((LOW_SENDS, HIGH_SENDS)):

            @pl.when((z >= 4) == (near == 1))
            def _(near=near, sends=sends):
                start(sends[part], met[near])

    met = (set(), set())

    build(0)
    send_part(0)
    build(1)
    send_part(1)
    recv[z * 8] = send[z * 4, c]

    lens = jnp.broadcast_to(len_ref[...], (16, HD))
    earlier = (iota((HD, HD), 0) < iota((HD, HD), 1)).astype(BF)
    starts = (
        jnp.dot((lens >> 8).astype(F32).astype(BF), earlier, preferred_element_type=F32) * 256.0
        + jnp.dot((lens & 255).astype(F32).astype(BF), earlier, preferred_element_type=F32))[0:1]
    starts = starts - ((me // 2) * CHIP).astype(F32)

    def mask(i, carry):
        row = (iota((256, HD), 0) + i * 256).astype(F32)
        first = jnp.max(jnp.where(starts <= row, starts, -1e9), axis=1, keepdims=True)
        rows = (iota((256, CHIP), 0) + i * 256).astype(F32)
        cols = iota((256, CHIP), 1).astype(F32)
        bias[pl.ds(i * 256, 256), :] = jnp.where((cols <= rows) & (cols >= first), 0.0, NEG)
        return carry

    lax.fori_loop(0, 3, mask, 0)

    block = (iota((64, HD), 0) & 15) >> 1
    for step in range(4):
        places = []
        for g in range(2):
            total = None
            for odd in range(2):
                zz = step // 2 * 4 + g * 2 + odd
                first = zz * 8 + step % 2 * 4
                for i in range(step % 2 * 4, step % 2 * 4 + 4):
                    if i > 0:
                        copy_of(zz, i, zz * 8 + i).wait_recv()
                    else:

                        @pl.when(zz != z)
                        def _(zz=zz):
                            copy_of(zz, 0, zz * 8).wait_recv()

                at = slice(g * 256 + odd * 64, g * 256 + odd * 64 + 64)
                at_left = slice(g * 256 + HD + odd * 64, g * 256 + HD + odd * 64 + 64)
                tail = recv[first:first + 4, :, 768:896]
                part = jnp.sum(tail.astype(F32), axis=0)
                total = part if total is None else total + part
                dense[at, :] = recv[first:first + 4, :, 0:768].reshape(64, 768)
                tail = tail.reshape(64, HD)
                for b in range(6):
                    dense[at_left, b * HD:(b + 1) * HD] = jnp.where(block == b, tail, jnp.zeros_like(tail))
            places.append(total[12:13] * 16.0 + total[13:14] - 16.0)
            places.append(total[14:15] * 16.0 + total[15:16] - 16.0)
        places = jnp.concatenate(places, axis=1).astype(I32)

        def deliver(i, carry, step=step, places=places):
            at = pl.ds(i * 256, 256)
            pick = (iota((256, 512), 0) + i * 256 == places).astype(F32).astype(BF)
            got = jnp.dot(pick, dense[...], preferred_element_type=F32).astype(BF)
            placed[at, :] = got if step == 0 else placed[at, :] + got
            return carry

        lax.fori_loop(0, 3, deliver, 0, unroll=True)

    scale = 1.0 / math.sqrt(HD)

    def attend(half, dst, dst_rows):
        upto = (half + 1) * ROWS
        rows = slice(half * ROWS, upto)
        for j in range(2):
            scores = lax.dot_general(
                placed[rows, j * HD:(j + 1) * HD], placed[0:upto, 256 + j * HD:256 + (j + 1) * HD],
                NT, preferred_element_type=F32) * scale + bias[rows, 0:upto]
            top = jnp.max(scores, axis=1, keepdims=True)
            weights = jnp.exp(scores - top)
            total = jnp.sum(weights, axis=1, keepdims=True)
            mix = jnp.dot(weights.astype(BF), placed[0:upto, 512 + j * HD:512 + (j + 1) * HD], preferred_element_type=F32)
            dst[:, dst_rows + j * HD:dst_rows + (j + 1) * HD] = (mix / total).astype(BF)

    cols = pl.ds(pl.multiple_of(c * 256, 256), 256)
    swap = pltpu.make_async_remote_copy(
        src_ref=mixed, dst_ref=out_ref.at[:, cols], send_sem=swap_send, recv_sem=swap_recv,
        device_id=device(z, 1), device_id_type=MESH)
    for core in range(2):

        @pl.when(c == core)
        def _(core=core):
            attend(1 - core, mixed, 0)
            swap.start()
            attend(core, out_ref, core * 256)

    for zz in range(8):

        @pl.when(zz != z)
        def _(zz=zz):
            copy_of(zz, 0, z * 8).wait_send()

        for i in range(1, 8):
            copy_of(zz, i, z * 8 + i).wait_send()
    swap.wait()


def body(queries, keys, values, target_row, doc_lengths):
    vmem = pl.BlockSpec(memory_space=pltpu.VMEM)
    return pl.pallas_call(
        kernel,
        out_shape=jax.ShapeDtypeStruct(queries.shape, BF),
        in_specs=[pl.BlockSpec(memory_space=pl.ANY)] * 3 + [vmem] * 2,
        out_specs=vmem,
        scratch_shapes=[
            pltpu.VMEM(queries.shape, BF),
            pltpu.VMEM(queries.shape, BF),
            pltpu.VMEM(queries.shape, BF),
            pltpu.SemaphoreType.DMA((3,)),
            pltpu.VMEM((32, 2, 16, WIDE), BF),
            pltpu.VMEM((64, 16, WIDE), BF),
            pltpu.VMEM((CHIP, 768), BF),
            pltpu.VMEM((CHIP, CHIP), F32),
            pltpu.VMEM((512, 768), BF),
            pltpu.VMEM((ROWS, 256), BF),
            pltpu.SemaphoreType.REGULAR((8,)),
            pltpu.SemaphoreType.DMA((64,)),
            pltpu.SemaphoreType.DMA((64,)),
            pltpu.SemaphoreType.DMA,
            pltpu.SemaphoreType.DMA,
        ],
        compiler_params=pltpu.CompilerParams(collective_id=0, has_side_effects=True, vmem_limit_bytes=535 * 2**20 // 10),
    )(queries, keys, values, target_row.reshape(1, -1), doc_lengths.reshape(1, -1))


def solution(mesh):
    in_specs = (P("seq", "head"), P("seq", "head"), P("seq", "head"), P("seq"), P())
    return jax.shard_map(body, mesh=mesh, in_specs=in_specs, out_specs=P("seq", "head"), check_vma=False)
```

```python
import functools
import math

import jax
import jax.numpy as jnp
from jax import lax
from jax.experimental import pallas as pl
from jax.experimental.pallas import tpu as pltpu
from jax.sharding import PartitionSpec as P

HD = 128
ROWS = 384
CAP = 9
CHIP = 2 * ROWS
NZ, NX = 8, 4
NEG = -1e30
MESH = pl.DeviceIdType.MESH
BF = jnp.bfloat16
F32 = jnp.float32
I32 = jnp.int32
WIDE = 7 * HD


def spread(zs, first=0, last=8):
    return [(zz, i) for i in range(first, last) for zz in zs]


def mixed_with(a, b):
    short, long = sorted((a, b), key=len)
    out = []
    for n, each in enumerate(long):
        out.append(each)
        out += short[n * len(short) // len(long):(n + 1) * len(short) // len(long)]
    return out


LOW_SENDS = tuple([(zz, i) for zz in zs for i in range(8)] for zs in ((0, 1), (2, 3), (4, 5, 6, 7)))
HIGH_SENDS = (
    spread((0, 1), 0, 2),
    spread((3, 2), 0, 2),
    mixed_with(spread((0, 3, 1, 2), 2), spread((4, 7, 5, 6))),
)
NT = (((1,), (1,)), ((), ()))


def iota(shape, dim):
    return lax.broadcasted_iota(I32, shape, dim)


def kernel(q_hbm, k_hbm, v_hbm, t_ref, len_ref, out_ref, q_ref, k_ref, v_ref, in_sem, send, recv, placed, bias, dense, mixed, ready, send_sem, recv_sem, swap_send, swap_recv):
    me = lax.axis_index("seq")
    head = lax.axis_index("head")
    z, x, c = me // 8, (me // 2) % 4, me % 2

    def device(zz, i):
        return (zz * 8 + ((x + i // 2) % 4) * 2 + (c + i % 2) % 2, head)

    pairs = ((q_hbm, q_ref), (k_hbm, k_ref), (v_hbm, v_ref))
    fetch = [pltpu.make_async_copy(src, dst, in_sem.at[i]) for i, (src, dst) in enumerate(pairs)]
    for copy in fetch:
        copy.start()

    barrier = pltpu.get_barrier_semaphore()
    for i in range(1, 8):
        pl.semaphore_signal(barrier, inc=1, device_id=device(z, i), device_id_type=MESH)
    for zz in range(1, 8):

        @pl.when(zz > z)
        def _(zz=zz):
            for i in range(8):
                pl.semaphore_signal(barrier, inc=1, device_id=device(zz, i), device_id_type=MESH)

    t = t_ref[...]
    dev = jnp.floor((t.astype(F32) + 0.5) * (1.0 / ROWS)).astype(I32)
    local = t - dev * ROWS
    rxv = (((dev >> 1) & 3) - x) & 3
    cc = dev & 1
    m = (dev >> 3) * 4 + rxv
    flags = iota((64, ROWS), 0) == m * 2 + cc
    before = (iota((ROWS, ROWS), 0) < iota((ROWS, ROWS), 1)).astype(BF)
    cum = jnp.dot(flags.astype(F32).astype(BF), before, preferred_element_type=F32)
    rank = jnp.sum(jnp.where(flags, cum, 0.0), axis=0, keepdims=True).astype(I32)
    s = cc * CAP + rank
    place = cc * ROWS + local
    hi, lo = ((place >> 4) + 1).astype(F32), (place & 15).astype(F32)
    over = s >= 16
    main_row = jnp.where(over, -1, m * 16 + s)
    left_row = jnp.where(over, m * 16 + s - 16, -1000)
    place_row = m * 16 + jnp.where(over, 14, 12)
    pl.semaphore_wait(barrier, z * 8 + 7)
    for zz in range(7):

        @pl.when(zz < z)
        def _(zz=zz):
            pl.semaphore_signal(ready.at[z], inc=1, device_id=device(zz, 0), device_id_type=MESH)

    lanes = iota((HD, ROWS), 0)
    hot = []
    for core in range(2):
        kk = rxv * 2 + ((c + core) & 1)
        kk = (kk & 3) + 4 * (z % 2)
        main_hot = lanes == kk * 16 + s
        left_hot = ((lanes >> 4) == kk) & ((lanes & 15) < 12) & ((lanes & 1) == s - 16)
        hot.append(jnp.where(over, left_hot.astype(F32), main_hot.astype(F32)).astype(BF))
    hot = jnp.concatenate(hot, axis=0)

    for copy in fetch:
        copy.wait()

    def build(chunk):
        rows = iota((128, ROWS), 0) + chunk * 128
        pick = (rows == main_row).astype(F32).astype(BF)
        at = pl.ds(chunk * 8, 8)
        left = lax.dot_general(
            (jnp.where(rows == place_row, hi, 0.0) + jnp.where(rows == place_row + 1, lo, 0.0)).astype(BF),
            hot, NT, preferred_element_type=F32)
        for a, ref in enumerate((q_ref, k_ref, v_ref)):
            got = jnp.dot(pick, ref[...], preferred_element_type=F32).astype(BF)
            for core in range(2):
                send[at, core, :, a * 256:(a + 1) * 256] = got[:, core * 256:(core + 1) * 256].reshape(8, 16, 256)
            for j in range(2):
                b = a * 2 + j
                pick_left = (rows - 2 * b == left_row).astype(F32).astype(BF)
                both = jnp.concatenate([ref[:, j * HD:(j + 1) * HD], ref[:, 256 + j * HD:256 + (j + 1) * HD]], axis=1)
                left = left + jnp.dot(pick_left, both, preferred_element_type=F32)
        left = left.astype(BF)
        for core in range(2):
            send[at, core, :, 768:896] = left[:, core * HD:(core + 1) * HD].reshape(8, 16, HD)

    def copy_of(zz, i, slot):
        return pltpu.make_async_remote_copy(
            src_ref=send.at[zz * 4 + i // 2, (c + i % 2) % 2], dst_ref=recv.at[slot],
            send_sem=send_sem.at[zz * 8 + i], recv_sem=recv_sem.at[slot],
            device_id=device(zz, i), device_id_type=MESH)

    def start(sends, greeted):
        for zz, i in sends:
            if zz > 0 and zz not in greeted:
                greeted.add(zz)

                @pl.when(zz > z)
                def _(zz=zz):
                    pl.semaphore_wait(ready.at[zz], 1)

            if i > 0:
                copy_of(zz, i, z * 8 + i).start()
            else:

                @pl.when(zz != z)
                def _(zz=zz):
                    copy_of(zz, 0, z * 8).start()

    def send_part(part):
        for near, sends in enumerate((LOW_SENDS, HIGH_SENDS)):

            @pl.when((z >= 4) == (near == 1))
            def _(near=near, sends=sends):
                start(sends[part], met[near])

    met = (set(), set())

    build(0)
    send_part(0)
    build(1)
    send_part(1)
    build(2)
    build(3)
    send_part(2)
    recv[z * 8] = send[z * 4, c]

    lens = jnp.broadcast_to(len_ref[...], (16, HD))
    earlier = (iota((HD, HD), 0) < iota((HD, HD), 1)).astype(BF)
    starts = (
        jnp.dot((lens >> 8).astype(F32).astype(BF), earlier, preferred_element_type=F32) * 256.0
        + jnp.dot((lens & 255).astype(F32).astype(BF), earlier, preferred_element_type=F32))[0:1]
    starts = starts - ((me // 2) * CHIP).astype(F32)

    def mask(i, carry):
        row = (iota((256, HD), 0) + i * 256).astype(F32)
        first = jnp.max(jnp.where(starts <= row, starts, -1e9), axis=1, keepdims=True)
        rows = (iota((256, CHIP), 0) + i * 256).astype(F32)
        cols = iota((256, CHIP), 1).astype(F32)
        bias[pl.ds(i * 256, 256), :] = jnp.where((cols <= rows) & (cols >= first), 0.0, NEG)
        return carry

    lax.fori_loop(0, 3, mask, 0)

    block = (iota((64, HD), 0) & 15) >> 1
    for step in range(4):
        places = []
        for g in range(2):
            total = None
            for odd in range(2):
                zz = step // 2 * 4 + g * 2 + odd
                first = zz * 8 + step % 2 * 4
                for i in range(step % 2 * 4, step % 2 * 4 + 4):
                    if i > 0:
                        copy_of(zz, i, zz * 8 + i).wait_recv()
                    else:

                        @pl.when(zz != z)
                        def _(zz=zz):
                            copy_of(zz, 0, zz * 8).wait_recv()

                at = slice(g * 256 + odd * 64, g * 256 + odd * 64 + 64)
                at_left = slice(g * 256 + HD + odd * 64, g * 256 + HD + odd * 64 + 64)
                tail = recv[first:first + 4, :, 768:896]
                part = jnp.sum(tail.astype(F32), axis=0)
                total = part if total is None else total + part
                dense[at, :] = recv[first:first + 4, :, 0:768].reshape(64, 768)
                tail = tail.reshape(64, HD)
                for b in range(6):
                    dense[at_left, b * HD:(b + 1) * HD] = jnp.where(block == b, tail, jnp.zeros_like(tail))
            places.append(total[12:13] * 16.0 + total[13:14] - 16.0)
            places.append(total[14:15] * 16.0 + total[15:16] - 16.0)
        places = jnp.concatenate(places, axis=1).astype(I32)

        def deliver(i, carry, step=step, places=places):
            at = pl.ds(i * 256, 256)
            pick = (iota((256, 512), 0) + i * 256 == places).astype(F32).astype(BF)
            got = jnp.dot(pick, dense[...], preferred_element_type=F32).astype(BF)
            placed[at, :] = got if step == 0 else placed[at, :] + got
            return carry

        lax.fori_loop(0, 3, deliver, 0, unroll=True)

    scale = 1.0 / math.sqrt(HD)

    def attend(half, dst, dst_rows):
        upto = (half + 1) * ROWS
        rows = slice(half * ROWS, upto)
        for j in range(2):
            scores = lax.dot_general(
                placed[rows, j * HD:(j + 1) * HD], placed[0:upto, 256 + j * HD:256 + (j + 1) * HD],
                NT, preferred_element_type=F32) * scale + bias[rows, 0:upto]
            top = jnp.max(scores, axis=1, keepdims=True)
            weights = jnp.exp(scores - top)
            total = jnp.sum(weights, axis=1, keepdims=True)
            mix = jnp.dot(weights.astype(BF), placed[0:upto, 512 + j * HD:512 + (j + 1) * HD], preferred_element_type=F32)
            dst[:, dst_rows + j * HD:dst_rows + (j + 1) * HD] = (mix / total).astype(BF)

    cols = pl.ds(pl.multiple_of(c * 256, 256), 256)
    swap = pltpu.make_async_remote_copy(
        src_ref=mixed, dst_ref=out_ref.at[:, cols], send_sem=swap_send, recv_sem=swap_recv,
        device_id=device(z, 1), device_id_type=MESH)
    for core in range(2):

        @pl.when(c == core)
        def _(core=core):
            attend(1 - core, mixed, 0)
            swap.start()
            attend(core, out_ref, core * 256)

    for zz in range(8):

        @pl.when(zz != z)
        def _(zz=zz):
            copy_of(zz, 0, z * 8).wait_send()

        for i in range(1, 8):
            copy_of(zz, i, z * 8 + i).wait_send()
    swap.wait()


def body(queries, keys, values, target_row, doc_lengths):
    vmem = pl.BlockSpec(memory_space=pltpu.VMEM)
    return pl.pallas_call(
        kernel,
        out_shape=jax.ShapeDtypeStruct(queries.shape, BF),
        in_specs=[pl.BlockSpec(memory_space=pl.ANY)] * 3 + [vmem] * 2,
        out_specs=vmem,
        scratch_shapes=[
            pltpu.VMEM(queries.shape, BF),
            pltpu.VMEM(queries.shape, BF),
            pltpu.VMEM(queries.shape, BF),
            pltpu.SemaphoreType.DMA((3,)),
            pltpu.VMEM((32, 2, 16, WIDE), BF),
            pltpu.VMEM((64, 16, WIDE), BF),
            pltpu.VMEM((CHIP, 768), BF),
            pltpu.VMEM((CHIP, CHIP), F32),
            pltpu.VMEM((512, 768), BF),
            pltpu.VMEM((ROWS, 256), BF),
            pltpu.SemaphoreType.REGULAR((8,)),
            pltpu.SemaphoreType.DMA((64,)),
            pltpu.SemaphoreType.DMA((64,)),
            pltpu.SemaphoreType.DMA,
            pltpu.SemaphoreType.DMA,
        ],
        compiler_params=pltpu.CompilerParams(collective_id=0, has_side_effects=True, vmem_limit_bytes=535 * 2**20 // 10),
    )(queries, keys, values, target_row.reshape(1, -1), doc_lengths.reshape(1, -1))


def solution(mesh):
    in_specs = (P("seq", "head"), P("seq", "head"), P("seq", "head"), P("seq"), P())
    return jax.shard_map(body, mesh=mesh, in_specs=in_specs, out_specs=P("seq", "head"), check_vma=False)
```

```python
import functools
import math

import jax
import jax.numpy as jnp
from jax import lax
from jax.experimental import pallas as pl
from jax.experimental.pallas import tpu as pltpu
from jax.sharding import PartitionSpec as P

HD = 128
ROWS = 384
CAP = 9
CHIP = 2 * ROWS
NZ, NX = 8, 4
NEG = -1e30
MESH = pl.DeviceIdType.MESH
BF = jnp.bfloat16
F32 = jnp.float32
I32 = jnp.int32
WIDE = 7 * HD


def spread(zs, first=0, last=8):
    return [(zz, i) for i in range(first, last) for zz in zs]


LOW_SENDS = tuple([(zz, i) for zz in zs for i in range(8)] for zs in ((0, 1), (2, 3), (4, 5, 6, 7)))
HIGH_SENDS = (
    spread((0, 1), 0, 2),
    spread((3, 2), 0, 2),
    spread((0, 3, 1, 2), 2) + spread((4, 7, 5, 6)),
)
NT = (((1,), (1,)), ((), ()))


def iota(shape, dim):
    return lax.broadcasted_iota(I32, shape, dim)


def kernel(q_hbm, k_hbm, v_hbm, t_ref, len_ref, out_ref, q_ref, k_ref, v_ref, in_sem, send, recv, placed, bias, dense, mixed, ready, send_sem, recv_sem, swap_send, swap_recv):
    me = lax.axis_index("seq")
    head = lax.axis_index("head")
    z, x, c = me // 8, (me // 2) % 4, me % 2

    def device(zz, i):
        return (zz * 8 + ((x + i // 2) % 4) * 2 + (c + i % 2) % 2, head)

    pairs = ((q_hbm, q_ref), (k_hbm, k_ref), (v_hbm, v_ref))
    fetch = [pltpu.make_async_copy(src, dst, in_sem.at[i]) for i, (src, dst) in enumerate(pairs)]
    for copy in fetch:
        copy.start()

    barrier = pltpu.get_barrier_semaphore()
    for i in range(1, 8):
        pl.semaphore_signal(barrier, inc=1, device_id=device(z, i), device_id_type=MESH)
    for zz in range(1, 8):

        @pl.when(zz > z)
        def _(zz=zz):
            for i in range(8):
                pl.semaphore_signal(barrier, inc=1, device_id=device(zz, i), device_id_type=MESH)

    t = t_ref[...]
    dev = jnp.floor((t.astype(F32) + 0.5) * (1.0 / ROWS)).astype(I32)
    local = t - dev * ROWS
    rxv = (((dev >> 1) & 3) - x) & 3
    cc = dev & 1
    m = (dev >> 3) * 4 + rxv
    flags = iota((64, ROWS), 0) == m * 2 + cc
    before = (iota((ROWS, ROWS), 0) < iota((ROWS, ROWS), 1)).astype(BF)
    cum = jnp.dot(flags.astype(F32).astype(BF), before, preferred_element_type=F32)
    rank = jnp.sum(jnp.where(flags, cum, 0.0), axis=0, keepdims=True).astype(I32)
    s = cc * CAP + rank
    place = cc * ROWS + local
    hi, lo = ((place >> 4) + 1).astype(F32), (place & 15).astype(F32)
    over = s >= 16
    main_row = jnp.where(over, -1, m * 16 + s)
    left_row = jnp.where(over, m * 16 + s - 16, -1000)
    place_row = m * 16 + jnp.where(over, 14, 12)
    pl.semaphore_wait(barrier, z * 8 + 7)
    for zz in range(7):

        @pl.when(zz < z)
        def _(zz=zz):
            pl.semaphore_signal(ready.at[z], inc=1, device_id=device(zz, 0), device_id_type=MESH)

    lanes = iota((HD, ROWS), 0)
    hot = []
    for core in range(2):
        kk = rxv * 2 + ((c + core) & 1)
        kk = (kk & 3) + 4 * (z % 2)
        main_hot = lanes == kk * 16 + s
        left_hot = ((lanes >> 4) == kk) & ((lanes & 15) < 12) & ((lanes & 1) == s - 16)
        hot.append(jnp.where(over, left_hot.astype(F32), main_hot.astype(F32)).astype(BF))
    hot = jnp.concatenate(hot, axis=0)

    for copy in fetch:
        copy.wait()

    def build(chunk):
        rows = iota((128, ROWS), 0) + chunk * 128
        pick = (rows == main_row).astype(F32).astype(BF)
        at = pl.ds(chunk * 8, 8)
        left = lax.dot_general(
            (jnp.where(rows == place_row, hi, 0.0) + jnp.where(rows == place_row + 1, lo, 0.0)).astype(BF),
            hot, NT, preferred_element_type=F32)
        for a, ref in enumerate((q_ref, k_ref, v_ref)):
            got = jnp.dot(pick, ref[...], preferred_element_type=F32).astype(BF)
            for core in range(2):
                send[at, core, :, a * 256:(a + 1) * 256] = got[:, core * 256:(core + 1) * 256].reshape(8, 16, 256)
            for j in range(2):
                b = a * 2 + j
                pick_left = (rows - 2 * b == left_row).astype(F32).astype(BF)
                both = jnp.concatenate([ref[:, j * HD:(j + 1) * HD], ref[:, 256 + j * HD:256 + (j + 1) * HD]], axis=1)
                left = left + jnp.dot(pick_left, both, preferred_element_type=F32)
        left = left.astype(BF)
        for core in range(2):
            send[at, core, :, 768:896] = left[:, core * HD:(core + 1) * HD].reshape(8, 16, HD)

    def copy_of(zz, i, slot):
        return pltpu.make_async_remote_copy(
            src_ref=send.at[zz * 4 + i // 2, (c + i % 2) % 2], dst_ref=recv.at[slot],
            send_sem=send_sem.at[zz * 8 + i], recv_sem=recv_sem.at[slot],
            device_id=device(zz, i), device_id_type=MESH)

    def start(sends, greeted):
        for zz, i in sends:
            if zz > 0 and zz not in greeted:
                greeted.add(zz)

                @pl.when(zz > z)
                def _(zz=zz):
                    pl.semaphore_wait(ready.at[zz], 1)

            if i > 0:
                copy_of(zz, i, z * 8 + i).start()
            else:

                @pl.when(zz != z)
                def _(zz=zz):
                    copy_of(zz, 0, z * 8).start()

    def send_part(part):
        for near, sends in enumerate((LOW_SENDS, HIGH_SENDS)):

            @pl.when((z >= 4) == (near == 1))
            def _(near=near, sends=sends):
                start(sends[part], met[near])

    met = (set(), set())

    build(0)
    send_part(0)
    build(1)
    send_part(1)
    build(2)
    build(3)
    send_part(2)
    recv[z * 8] = send[z * 4, c]

    lens = jnp.broadcast_to(len_ref[...], (16, HD))
    earlier = (iota((HD, HD), 0) < iota((HD, HD), 1)).astype(BF)
    starts = (
        jnp.dot((lens >> 8).astype(F32).astype(BF), earlier, preferred_element_type=F32) * 256.0
        + jnp.dot((lens & 255).astype(F32).astype(BF), earlier, preferred_element_type=F32))[0:1]
    starts = starts - ((me // 2) * CHIP).astype(F32)

    def mask(i, carry):
        row = (iota((256, HD), 0) + i * 256).astype(F32)
        first = jnp.max(jnp.where(starts <= row, starts, -1e9), axis=1, keepdims=True)
        rows = (iota((256, CHIP), 0) + i * 256).astype(F32)
        cols = iota((256, CHIP), 1).astype(F32)
        bias[pl.ds(i * 256, 256), :] = jnp.where((cols <= rows) & (cols >= first), 0.0, NEG)
        return carry

    lax.fori_loop(0, 3, mask, 0)

    block = (iota((64, HD), 0) & 15) >> 1
    for step in range(4):
        places = []
        for g in range(2):
            total = None
            for odd in range(2):
                zz = step // 2 * 4 + g * 2 + odd
                first = zz * 8 + step % 2 * 4
                for i in range(step % 2 * 4, step % 2 * 4 + 4):
                    if i > 0:
                        copy_of(zz, i, zz * 8 + i).wait_recv()
                    else:

                        @pl.when(zz != z)
                        def _(zz=zz):
                            copy_of(zz, 0, zz * 8).wait_recv()

                at = slice(g * 256 + odd * 64, g * 256 + odd * 64 + 64)
                at_left = slice(g * 256 + HD + odd * 64, g * 256 + HD + odd * 64 + 64)
                tail = recv[first:first + 4, :, 768:896]
                part = jnp.sum(tail.astype(F32), axis=0)
                total = part if total is None else total + part
                dense[at, :] = recv[first:first + 4, :, 0:768].reshape(64, 768)
                tail = tail.reshape(64, HD)
                for b in range(6):
                    dense[at_left, b * HD:(b + 1) * HD] = jnp.where(block == b, tail, jnp.zeros_like(tail))
            places.append(total[12:13] * 16.0 + total[13:14] - 16.0)
            places.append(total[14:15] * 16.0 + total[15:16] - 16.0)
        places = jnp.concatenate(places, axis=1).astype(I32)

        def deliver(i, carry, step=step, places=places):
            at = pl.ds(i * 256, 256)
            pick = (iota((256, 512), 0) + i * 256 == places).astype(F32).astype(BF)
            got = jnp.dot(pick, dense[...], preferred_element_type=F32).astype(BF)
            placed[at, :] = got if step == 0 else placed[at, :] + got
            return carry

        lax.fori_loop(0, 3, deliver, 0, unroll=True)

    scale = 1.0 / math.sqrt(HD)

    def attend(half, dst, dst_rows):
        upto = (half + 1) * ROWS
        rows = slice(half * ROWS, upto)
        for j in range(2):
            scores = lax.dot_general(
                placed[rows, j * HD:(j + 1) * HD], placed[0:upto, 256 + j * HD:256 + (j + 1) * HD],
                NT, preferred_element_type=F32) * scale + bias[rows, 0:upto]
            top = jnp.max(scores, axis=1, keepdims=True)
            weights = jnp.exp(scores - top)
            total = jnp.sum(weights, axis=1, keepdims=True)
            mix = jnp.dot(weights.astype(BF), placed[0:upto, 512 + j * HD:512 + (j + 1) * HD], preferred_element_type=F32)
            dst[:, dst_rows + j * HD:dst_rows + (j + 1) * HD] = (mix / total).astype(BF)

    cols = pl.ds(pl.multiple_of(c * 256, 256), 256)
    swap = pltpu.make_async_remote_copy(
        src_ref=mixed, dst_ref=out_ref.at[:, cols], send_sem=swap_send, recv_sem=swap_recv,
        device_id=device(z, 1), device_id_type=MESH)
    for core in range(2):

        @pl.when(c == core)
        def _(core=core):
            attend(1 - core, mixed, 0)
            swap.start()
            attend(core, out_ref, core * 256)

    for zz in range(8):

        @pl.when(zz != z)
        def _(zz=zz):
            copy_of(zz, 0, z * 8).wait_send()

        for i in range(1, 8):
            copy_of(zz, i, z * 8 + i).wait_send()
    swap.wait()


def body(queries, keys, values, target_row, doc_lengths):
    vmem = pl.BlockSpec(memory_space=pltpu.VMEM)
    return pl.pallas_call(
        kernel,
        out_shape=jax.ShapeDtypeStruct(queries.shape, BF),
        in_specs=[pl.BlockSpec(memory_space=pl.ANY)] * 3 + [vmem] * 2,
        out_specs=vmem,
        scratch_shapes=[
            pltpu.VMEM(queries.shape, BF),
            pltpu.VMEM(queries.shape, BF),
            pltpu.VMEM(queries.shape, BF),
            pltpu.SemaphoreType.DMA((3,)),
            pltpu.VMEM((32, 2, 16, WIDE), BF),
            pltpu.VMEM((64, 16, WIDE), BF),
            pltpu.VMEM((CHIP, 768), BF),
            pltpu.VMEM((CHIP, CHIP), F32),
            pltpu.VMEM((512, 768), BF),
            pltpu.VMEM((ROWS, 256), BF),
            pltpu.SemaphoreType.REGULAR((8,)),
            pltpu.SemaphoreType.DMA((64,)),
            pltpu.SemaphoreType.DMA((64,)),
            pltpu.SemaphoreType.DMA,
            pltpu.SemaphoreType.DMA,
        ],
        compiler_params=pltpu.CompilerParams(collective_id=0, has_side_effects=True, vmem_limit_bytes=535 * 2**20 // 10),
    )(queries, keys, values, target_row.reshape(1, -1), doc_lengths.reshape(1, -1))


def solution(mesh):
    in_specs = (P("seq", "head"), P("seq", "head"), P("seq", "head"), P("seq"), P())
    return jax.shard_map(body, mesh=mesh, in_specs=in_specs, out_specs=P("seq", "head"), check_vma=False)
```
